32 devices in a mesh: groups: 2 (over y), patch: 4 (over x, core), frame: 4 (over z).
Axes of the slice: x: 2, y: 2, z: 4, core: 2. Of those that a mesh axis runs over, the one named last changes fastest.
Arguments:
- layer_entry_activations: float32 [8, 512, 1152], P(('groups', 'frame'), 'patch'), parts along dimension 0, may hold values from -6 to 6
- planar_rmsnorm_multiplier: float32 [1152], replicated, may hold values from 0.25 to 1.75
- timewise_rmsnorm_multiplier: float32 [1152], replicated, may hold values from 0.25 to 1.75
- feedforward_rmsnorm_multiplier: float32 [1152], replicated, may hold values from 0.25 to 1.75
- planar_triple_matrix: bfloat16 [3, 1152, 1152], P(None, None, 'patch'), may hold values from -0.1875 to 0.1875
- planar_logit_factor: float32 [16], replicated, may hold values from 1 to 6
- planar_projection_matrix: bfloat16 [1152, 1152], replicated, may hold values from -0.1875 to 0.1875
- timewise_asker_content_matrix: bfloat16 [2, 1152, 1152], P(None, None, 'frame'), may hold values from -0.1875 to 0.1875
- timewise_lookup_codes: int32 [8, 512, 1152], P(('groups', 'frame'), 'patch'), parts along dimension 0, may hold values from -127 to 127
- lookup_quantum_factor: float32 [16], replicated, may hold values from 0.003 to 0.03
- timestep_ordinal: int32 [8], P('groups'), parts along dimension 0, may hold values from 0 to 255
- timewise_projection_matrix: bfloat16 [1152, 1152], replicated, may hold values from -0.1875 to 0.1875
- widening_matrix: bfloat16 [1152, 4608], P(None, 'patch'), may hold values from -0.1875 to 0.1875
- narrowing_matrix: bfloat16 [4608, 1152], P('patch'), may hold values from -0.09375 to 0.09375
Outputs:
- block_output: float32 [8, 512, 1152], P(('groups', 'frame'), 'patch'), parts along dimension 0
The draws below stay inside these ranges and needn't reach their ends.
There are 2 independent parts, one for each index of `groups`. The reference program is written for one: setup_inputs(seed, part) draws one part's arguments, and reference() takes and returns one part's arrays. A program takes and returns all parts, laid end to end along the dimension named above; an argument that names none is the same for every part. Nothing has to cross between parts.
All inputs are finite; a program needn't handle non-finite values.
Results may differ from the reference program's by a relative error of at most 0.0088.
Values may be sent and summed in bfloat16 or wider, within the bound.
A program may use at most 64 MiB of HBM per device.

```python
import math
import jax
import jax.numpy as jnp
from jax import lax

ATTENDER_TOTAL = 16
ATTENDER_WIDTH = 72
D = 1152
FF = 4608
F = 4
P_SIZE = 512


def set_ends(drawn, rng, least, high):
    index_at = [jax.random.randint(jax.random.fold_in(rng, axis), (), 0, length) for axis, length in enumerate(drawn.shape)]
    main_axis = drawn.shape.index(max(drawn.shape))
    next_to = index_at[:main_axis] + [(index_at[main_axis] + 1) % drawn.shape[main_axis]] + index_at[main_axis + 1:]
    return drawn.at[tuple(index_at)].set(least).at[tuple(next_to)].set(high)


def levels(key, shape, split, least, high):
    loudness, own = 1.0, jax.random.fold_in(key, 6)
    for dim, parts in split:
        steps = jnp.exp(jax.random.uniform(jax.random.fold_in(own, dim), (parts,), jnp.float32, least / len(split), high / len(split)))
        loudness = loudness * jnp.repeat(steps, shape[dim] // parts).reshape([-1 if axis == dim else 1 for axis in range(len(shape))])
    return loudness


def gaussian(stream_key, shape, deviation, reach, cuts=(), held_as=jnp.bfloat16):
    result = jax.random.normal(stream_key, shape, jnp.float32) * deviation
    if len(cuts) > 0:
        result = levels(stream_key, shape, cuts, -0.22, 0.18) * result
    return jnp.clip(result, min=-reach, max=reach).astype(held_as)


def setup_inputs(seed: int = 0, part: int = 0) -> dict:
    streams_of = jax.random.split(jax.random.key(seed), 15)
    part_keys = jax.random.split(jax.random.fold_in(streams_of[14], part), 15)
    return {
        "layer_entry_activations": gaussian(part_keys[0], (F, P_SIZE, D), 1.0, 6.0, ((0, 4), (1, 4)), jnp.float32),
        "planar_rmsnorm_multiplier": jnp.clip(1.0 + 0.15 * jax.random.normal(streams_of[1], (D,), jnp.float32), 0.25, 1.75),
        "timewise_rmsnorm_multiplier": jnp.clip(1.0 + 0.15 * jax.random.normal(streams_of[2], (D,), jnp.float32), 0.25, 1.75),
        "feedforward_rmsnorm_multiplier": jnp.clip(1.0 + 0.15 * jax.random.normal(streams_of[3], (D,), jnp.float32), 0.25, 1.75),
        "planar_triple_matrix": gaussian(streams_of[4], (3, D, D), D ** -0.5, 0.1875, ((2, 4),)),
        "planar_logit_factor": jnp.clip(jnp.exp(jax.random.uniform(streams_of[5], (ATTENDER_TOTAL,), jnp.float32, math.log(1.0), math.log(6.0))), 1.0, 6.0),
        "planar_projection_matrix": gaussian(streams_of[6], (D, D), D ** -0.5, 0.1875),
        "timewise_asker_content_matrix": gaussian(streams_of[7], (2, D, D), D ** -0.5, 0.1875, ((2, 4),)),
        "timewise_lookup_codes": set_ends(jax.random.randint(part_keys[8], (F, P_SIZE, D), -127, 128), jax.random.fold_in(part_keys[8], 1), -127, 127).astype(jnp.int32),
        "lookup_quantum_factor": jnp.clip(jnp.exp(jax.random.uniform(streams_of[9], (ATTENDER_TOTAL,), jnp.float32, math.log(0.003), math.log(0.03))), 0.003, 0.03),
        "timestep_ordinal": set_ends(jax.random.randint(part_keys[10], (F,), 0, 256), jax.random.fold_in(part_keys[10], 1), 0, 255).astype(jnp.int32),
        "timewise_projection_matrix": gaussian(streams_of[11], (D, D), D ** -0.5, 0.1875),
        "widening_matrix": gaussian(streams_of[12], (D, FF), D ** -0.5, 0.1875, ((1, 4),)),
        "narrowing_matrix": gaussian(streams_of[13], (FF, D), FF ** -0.5, 0.09375, ((0, 4),)),
    }


epsilon = 1e-06

def rms_scale(entries, gain_row):
    return entries * lax.rsqrt(lax.optimization_barrier(jnp.mean(entries * entries, axis=-1, keepdims=True)) + epsilon) * gain_row

def head_norm(entries):
    return entries * lax.rsqrt(lax.optimization_barrier(jnp.mean(entries * entries, axis=-1, keepdims=True)) + epsilon)

def frame_angles(positions_in, head_width):
    half_width = head_width // 2
    inverse = jnp.exp(jnp.arange(half_width, dtype=jnp.float32) * (-2.0 * math.log(10000.0) / head_width))
    return positions_in.astype(jnp.float32)[:, None] * inverse[None, :]

def rotate_pairs(entries, angles):
    half_width = entries.shape[-1] // 2
    first_half = entries[..., :half_width]
    second_half = entries[..., half_width:]
    cosine = jnp.cos(angles)
    sine_part = jnp.sin(angles)
    return jnp.concatenate([first_half * cosine - second_half * sine_part, second_half * cosine + first_half * sine_part], axis=-1)

def round_wide(entries):
    return lax.optimization_barrier(entries.astype(jnp.bfloat16)).astype(jnp.float32)

def reference(layer_entry_activations, planar_rmsnorm_multiplier, timewise_rmsnorm_multiplier, feedforward_rmsnorm_multiplier, planar_triple_matrix, planar_logit_factor, planar_projection_matrix, timewise_asker_content_matrix, timewise_lookup_codes, lookup_quantum_factor, timestep_ordinal, timewise_projection_matrix, widening_matrix, narrowing_matrix):
    frame_total, patch_total, model_width = layer_entry_activations.shape
    normed = rms_scale(layer_entry_activations, planar_rmsnorm_multiplier).astype(jnp.bfloat16)
    logit_multiplier = planar_logit_factor / math.sqrt(ATTENDER_WIDTH)

    def spatial_frame(frame_tokens):
        projected = [jnp.dot(frame_tokens, planar_triple_matrix[member], preferred_element_type=jnp.float32).reshape(patch_total, ATTENDER_TOTAL, ATTENDER_WIDTH) for member in range(3)]
        queries = round_wide(head_norm(projected[0]))
        keys_all = round_wide(head_norm(projected[1]))
        values_all = round_wide(projected[2])
        scores = jnp.einsum('qhe,khe->hqk', queries, keys_all) * logit_multiplier[:, None, None]
        weights = jnp.exp(scores)
        weights = round_wide(weights / lax.optimization_barrier(jnp.sum(weights, axis=-1, keepdims=True)))
        mixed_rows = jnp.einsum('hqk,khe->qhe', weights, values_all)
        return mixed_rows.reshape(patch_total, model_width).astype(jnp.bfloat16)
    attended = lax.map(spatial_frame, normed)
    flat_rows = attended.reshape(frame_total * patch_total, model_width)
    after_spatial = layer_entry_activations + jnp.dot(flat_rows, planar_projection_matrix, preferred_element_type=jnp.float32).reshape(layer_entry_activations.shape)
    normed = rms_scale(after_spatial, timewise_rmsnorm_multiplier).astype(jnp.bfloat16).reshape(frame_total * patch_total, model_width)
    angles = frame_angles(timestep_ordinal, ATTENDER_WIDTH)[:, None, None, :]
    queries = jnp.dot(normed, timewise_asker_content_matrix[0], preferred_element_type=jnp.float32).reshape(frame_total, patch_total, ATTENDER_TOTAL, ATTENDER_WIDTH)
    queries = round_wide(rotate_pairs(head_norm(queries), angles))
    values_all = round_wide(jnp.dot(normed, timewise_asker_content_matrix[1], preferred_element_type=jnp.float32).reshape(frame_total, patch_total, ATTENDER_TOTAL, ATTENDER_WIDTH))
    keys_all = timewise_lookup_codes.astype(jnp.float32).reshape(frame_total, patch_total, ATTENDER_TOTAL, ATTENDER_WIDTH) * lookup_quantum_factor[:, None]
    keys_all = round_wide(rotate_pairs(keys_all, angles))
    scores = jnp.einsum('fphe,gphe->phfg', queries, keys_all) / math.sqrt(ATTENDER_WIDTH)
    weights = jnp.exp(scores)
    weights = round_wide(weights / lax.optimization_barrier(jnp.sum(weights, axis=-1, keepdims=True)))
    mixed_rows = jnp.einsum('phfg,gphe->fphe', weights, values_all).reshape(frame_total * patch_total, model_width).astype(jnp.bfloat16)
    after_temporal = after_spatial + jnp.dot(mixed_rows, timewise_projection_matrix, preferred_element_type=jnp.float32).reshape(layer_entry_activations.shape)
    normed = rms_scale(after_temporal, feedforward_rmsnorm_multiplier).astype(jnp.bfloat16).reshape(frame_total * patch_total, model_width)
    hidden = jax.nn.gelu(jnp.dot(normed, widening_matrix, preferred_element_type=jnp.float32), approximate=False).astype(jnp.bfloat16)
    return after_temporal + jnp.dot(hidden, narrowing_matrix, preferred_element_type=jnp.float32).reshape(layer_entry_activations.shape)
```

```python
import functools
import math

import jax
import jax.numpy as jnp
import numpy as np
from jax import lax
from jax.experimental import pallas as pl
from jax.experimental.pallas import tpu as pltpu
from jax.sharding import PartitionSpec as P

HEADS = 16
HW = 72
EPS = 1e-6
BF = jnp.bfloat16
F32 = jnp.float32
MESH = pl.DeviceIdType.MESH


def dot(a, b):
    return jnp.dot(a, b, preferred_element_type=F32)


def split_dot(a, b):
    high = a.astype(BF)
    low = (a - high.astype(F32)).astype(BF)
    return dot(high, b) + dot(low, b)


def rms(v, g):
    return (v * lax.rsqrt(jnp.mean(v * v, axis=-1, keepdims=True) + EPS) * g).astype(BF)


def hnorm(u, same):
    return u * lax.rsqrt(split_dot(u * u, same) * (1.0 / HW) + EPS)


def kernel(
    dims,
    logit_ref, quantum_ref, step_ref,
    x_hbm, codes_hbm, gs_ref, gt_ref, gm_ref,
    same_s_ref, same_t_ref, swap_ref, inv_ref, sign_ref,
    wqkv_hbm, wps_hbm, wqv_hbm, wpt_hbm, w1_hbm, w2_hbm,
    out_ref,
    x, codes, wqkv, wps, wqv, wpt, w1, w2, load_sem,
    tok_a, qs, ks, vs, att, att_in,
    kt_out, kt, tok_t, qt, vt, att_t, att_t_in,
    after, tok_m, sib_out, sib_in, x_out, x_in,
    a_send, a_recv, af_send,
    s_send, s_recv, k_send, k_recv,
    tl_send, tl_recv, tr_send, tr_recv, t_send, t_recv,
    m_send, m_recv, mf_send, b_send, b_recv, c_send, c_recv,
):
    n_p, n_f, rows, chunks, cs, ct = dims
    n_x = n_p // 2
    me_g = lax.axis_index("groups")
    me_p = lax.axis_index("patch")
    me_f = lax.axis_index("frame")
    chip = lax.div(me_p, 2)
    core = lax.rem(me_p, 2)
    sib = me_p + 1 - 2 * core
    step_rows = rows // chunks

    def patch_dev(j):
        return (me_g, j, me_f)

    def frame_dev(j):
        return (me_g, me_p, j)

    loads = []
    for n, (src, dst) in enumerate(
        [(x_hbm, x), (codes_hbm, codes), (wqkv_hbm, wqkv), (wps_hbm, wps),
         (wqv_hbm, wqv), (wpt_hbm, wpt), (w1_hbm, w1), (w2_hbm, w2)]
    ):
        copy = pltpu.make_async_copy(src, dst, load_sem.at[n])
        copy.start()
        loads.append(copy)

    barrier = pltpu.get_barrier_semaphore()
    for d in range(1, n_p):
        pl.semaphore_signal(barrier, 1, device_id=patch_dev(lax.rem(me_p + d, n_p)), device_id_type=MESH)
    for d in range(1, n_f):
        pl.semaphore_signal(barrier, 1, device_id=frame_dev(lax.rem(me_f + d, n_f)), device_id_type=MESH)

    pending = []

    def send(src, dst, ssem, rsem, dev):
        copy = pltpu.make_async_remote_copy(
            src_ref=src, dst_ref=dst, send_sem=ssem, recv_sem=rsem,
            device_id=dev, device_id_type=MESH)
        copy.start()
        return copy

    def arrived(ref, rsem, ssem):
        pltpu.make_async_remote_copy(
            src_ref=ref, dst_ref=ref, send_sem=ssem, recv_sem=rsem,
            device_id=patch_dev(sib), device_id_type=MESH).wait_recv()

    def cut(c):
        return pl.ds(c * step_rows, step_rows)

    def gather_own(tok, ssem, rsem):
        for d in range(1, n_x):
            there = lax.rem(chip + d, n_x) * 2 + core
            for c in range(chunks):
                ref = tok.at[me_p, cut(c)]
                pending.append(send(ref, ref, ssem.at[d, c], rsem.at[me_p, c], patch_dev(there)))
        for c in range(chunks):
            ref = tok.at[me_p, cut(c)]
            pending.append(send(ref, ref, ssem.at[0, c], rsem.at[me_p, c], patch_dev(sib)))

    def wait_shard(tok, j, rsem, ssem):
        for c in range(chunks):
            arrived(tok.at[j, cut(c)], rsem.at[j, c], ssem.at[0, c])

    def forward(tok, d, ssem, rsem, fsem):
        j = lax.rem(chip + d, n_x) * 2 + core
        for c in range(chunks):
            ref = tok.at[j, cut(c)]
            arrived(ref, rsem.at[j, c], ssem.at[0, c])
            pending.append(send(ref, ref, fsem.at[d, c], rsem.at[j, c], patch_dev(sib)))

    loads[0].wait()
    tok_a[pl.ds(me_p, 1)] = rms(x[...], gs_ref[...])[None]
    pl.semaphore_wait(barrier, n_p - 1 + n_f - 1)
    gather_own(tok_a, a_send, a_recv)

    loads[1].wait()
    same_t = same_t_ref[...]
    swap = swap_ref[...]
    head_t = lax.broadcasted_iota(jnp.int32, (1, ct), 1)

    def angles(j):
        a = step_ref[j].astype(F32) * inv_ref[...]
        return jnp.cos(a), jnp.sin(a) * sign_ref[...]

    cos_me, sin_me = angles(me_f)
    heads_t = ct // HW
    for j in range(n_f):
        u = codes[:, j * ct:(j + 1) * ct].astype(F32).astype(BF)
        scale = jnp.zeros((1, ct), F32)
        for h in range(heads_t):
            scale = jnp.where((head_t >= h * HW) & (head_t < (h + 1) * HW), quantum_ref[j * heads_t + h], scale)
        turned = u.astype(F32) * scale * cos_me + dot(u, swap) * scale * sin_me
        kt_out[j] = turned.astype(BF)
    for d in range(1, n_f):
        j = lax.rem(me_f + d, n_f)
        pending.append(send(kt_out.at[j], kt.at[me_f], k_send.at[d], k_recv.at[me_f], frame_dev(j)))
    kt[pl.ds(me_f, 1)] = kt_out[pl.ds(me_f, 1)]

    same_s = same_s_ref[...]
    loads[2].wait()

    def pair(ref, xc):
        return ref[pl.ds(xc * 2, 2)].reshape(2 * rows, ref.shape[-1])

    def project(xc):
        t = pair(tok_a, xc)
        qs[pl.ds(xc * 2, 2)] = hnorm(dot(t, wqkv[0]), same_s).astype(BF).reshape(2, rows, cs)
        ks[pl.ds(xc * 2, 2)] = hnorm(dot(t, wqkv[1]), same_s).astype(BF).reshape(2, rows, cs)
        vs[pl.ds(xc * 2, 2)] = dot(t, wqkv[2]).astype(BF).reshape(2, rows, cs)

    wait_shard(tok_a, sib, a_recv, a_send)
    project(chip)
    for d in range(1, n_x):
        forward(tok_a, d, a_send, a_recv, af_send)
    for d in range(1, n_x):
        xc = lax.rem(chip + d, n_x)
        wait_shard(tok_a, xc * 2 + 1 - core, a_recv, a_send)
        project(xc)

    head_s = lax.broadcasted_iota(jnp.int32, (1, cs), 1)
    heads_s = cs // HW
    k_all = ks[...].reshape(n_p * rows, cs)
    v_all = vs[...].reshape(n_p * rows, cs)

    def attend(xc):
        q = pair(qs, xc)
        mixed = jnp.zeros((2 * rows, cs), F32)
        for h in range(heads_s):
            mine = (head_s >= h * HW) & (head_s < (h + 1) * HW)
            qh = jnp.where(mine, q, jnp.zeros_like(q))
            s = lax.dot_general(qh, k_all, (((1,), (1,)), ((), ())), preferred_element_type=F32)
            e = jnp.exp(s * (logit_ref[me_p * heads_s + h] * (1.0 / math.sqrt(HW))))
            p = (e * (1.0 / jnp.sum(e, axis=-1, keepdims=True))).astype(BF)
            mixed = jnp.where(mine, dot(p, v_all), mixed)
        att[pl.ds(xc * 2, 2)] = mixed.astype(BF).reshape(2, rows, cs)

    for d in range(1, n_x):
        xc = lax.rem(chip + d, n_x)
        attend(xc)
        for b in range(2):
            j = xc * 2 + b
            pending.append(send(att.at[j], att_in.at[me_p], s_send.at[2 * d + b], s_recv.at[me_p], patch_dev(j)))
    attend(chip)
    pending.append(send(att.at[sib], att_in.at[me_p], s_send.at[0], s_recv.at[me_p], patch_dev(sib)))
    att_in[pl.ds(me_p, 1)] = att[pl.ds(me_p, 1)]
    loads[3].wait()
    for d in range(1, n_p):
        j = lax.rem(me_p + d, n_p)
        arrived(att_in.at[j], s_recv.at[j], s_send.at[0])
    total = x[...]
    for j in range(n_p):
        total = total + dot(att_in[j], wps[j])
    after[...] = total

    tok_t[pl.ds(me_f, 1)] = rms(total, gt_ref[...])[None]
    has_right = me_f + 1 < n_f
    has_left = me_f > 0
    late = []

    def pass_on(j, c, t, right):
        ref = tok_t.at[j, cut(c)]
        if right:
            return pltpu.make_async_remote_copy(
                src_ref=ref, dst_ref=ref, send_sem=tr_send.at[t, c], recv_sem=tr_recv.at[t, c],
                device_id=frame_dev(jnp.minimum(me_f + 1, n_f - 1)), device_id_type=MESH)
        return pltpu.make_async_remote_copy(
            src_ref=ref, dst_ref=ref, send_sem=tl_send.at[t, c], recv_sem=tl_recv.at[t, c],
            device_id=frame_dev(jnp.maximum(me_f - 1, 0)), device_id_type=MESH)

    for c in range(chunks):
        @pl.when(has_right)
        def _():
            pass_on(me_f, c, 0, True).start()

        @pl.when(has_left)
        def _():
            pass_on(me_f, c, 0, False).start()

    loads[4].wait()

    def project_t(j):
        t = tok_t[pl.ds(j, 1)].reshape(rows, tok_t.shape[-1])
        u = hnorm(dot(t, wqv[0]), same_t)
        cos_j, sin_j = angles(j)
        qt[pl.ds(j, 1)] = (u * cos_j + split_dot(u, swap) * sin_j).astype(BF)[None]
        vt[pl.ds(j, 1)] = dot(t, wqv[1]).astype(BF)[None]

    project_t(me_f)
    for t in range(1, n_f):
        from_left = me_f >= t
        from_right = me_f + t < n_f
        for c in range(chunks):
            @pl.when(from_left)
            def _():
                pass_on(jnp.maximum(me_f - t, 0), c, t - 1, True).wait_recv()

            if t < n_f - 1:
                @pl.when(from_left & has_right)
                def _():
                    pass_on(jnp.maximum(me_f - t, 0), c, t, True).start()

            @pl.when(from_right)
            def _():
                pass_on(jnp.minimum(me_f + t, n_f - 1), c, t - 1, False).wait_recv()

            if t < n_f - 1:
                @pl.when(from_right & has_left)
                def _():
                    pass_on(jnp.minimum(me_f + t, n_f - 1), c, t, False).start()

        @pl.when(from_left)
        def _():
            project_t(jnp.maximum(me_f - t, 0))

        @pl.when(from_right)
        def _():
            project_t(jnp.minimum(me_f + t, n_f - 1))

    for d in range(1, n_f):
        j = lax.rem(me_f + d, n_f)
        arrived(kt.at[j], k_recv.at[j], k_send.at[d])

    for d in sorted(range(n_f), key=lambda d: -min(d, n_f - d)):
        j = lax.rem(me_f + d, n_f)
        q = qt[pl.ds(j, 1)].reshape(rows, ct).astype(F32)
        prods = jnp.concatenate([q * kt[g].astype(F32) for g in range(n_f)], axis=0)
        e = jnp.exp(split_dot(prods, same_t) * (1.0 / math.sqrt(HW))).reshape(n_f, rows, ct)
        bottom = e[0]
        for g in range(1, n_f):
            bottom = bottom + e[g]
        inverse = 1.0 / bottom
        mixed = jnp.zeros((rows, ct), F32)
        for g in range(n_f):
            mixed = mixed + (e[g] * inverse).astype(BF).astype(F32) * vt[g].astype(F32)
        if d == 0:
            att_t_in[pl.ds(me_f, 1)] = mixed.astype(BF)[None]
        else:
            att_t[d] = mixed.astype(BF)
            pending.append(send(att_t.at[d], att_t_in.at[me_f], t_send.at[d], t_recv.at[me_f], frame_dev(j)))

    loads[5].wait()
    for d in range(1, n_f):
        j = lax.rem(me_f + d, n_f)
        arrived(att_t_in.at[j], t_recv.at[j], t_send.at[d])
    total = after[...]
    for j in range(n_f):
        total = total + dot(att_t_in[j], wpt[j])
    after[...] = total

    tok_m[pl.ds(me_p, 1)] = rms(total, gm_ref[...])[None]
    gather_own(tok_m, m_send, m_recv)
    loads[6].wait()
    loads[7].wait()

    def mlp(xc):
        u = dot(pair(tok_m, xc), w1[...])
        hidden = (0.5 * u * (1.0 + lax.erf(u * (1.0 / math.sqrt(2.0))))).astype(BF)
        return dot(hidden, w2[...])

    def part(both, which):
        return jnp.where(which == 0, both[:rows], both[rows:])

    wait_shard(tok_m, sib, m_recv, m_send)
    both = mlp(chip)
    sib_out[0] = part(both, 1 - core).astype(BF)
    pending.append(send(sib_out.at[0], sib_in.at[0], b_send.at[0], b_recv.at[0], patch_dev(sib)))
    after[...] = after[...] + part(both, core)
    for d in range(1, n_x):
        forward(tok_m, d, m_send, m_recv, mf_send)
    for d in range(1, n_x):
        xc = lax.rem(chip + d, n_x)
        wait_shard(tok_m, xc * 2 + 1 - core, m_recv, m_send)
        both = mlp(xc)
        sib_out[d] = part(both, 1 - core).astype(BF)
        pending.append(send(sib_out.at[d], sib_in.at[d], b_send.at[d], b_recv.at[d], patch_dev(sib)))
        arrived(sib_in.at[d], b_recv.at[d], b_send.at[d])
        x_out[d] = (part(both, core) + sib_in[d].astype(F32)).astype(BF)
        pending.append(send(x_out.at[d], x_in.at[d], c_send.at[d], c_recv.at[d], patch_dev(xc * 2 + core)))
    arrived(sib_in.at[0], b_recv.at[0], b_send.at[0])
    total = after[...] + sib_in[0].astype(F32)
    for d in range(1, n_x):
        arrived(x_in.at[d], c_recv.at[d], c_send.at[d])
        total = total + x_in[d].astype(F32)
    out_ref[...] = total

    for copy in pending:
        copy.wait_send()
    for t in range(n_f - 1):
        for c in range(chunks):
            @pl.when((me_f >= t) & has_right)
            def _():
                pass_on(jnp.maximum(me_f - t, 0), c, t, True).wait_send()

            @pl.when((me_f + t < n_f) & has_left)
            def _():
                pass_on(jnp.minimum(me_f + t, n_f - 1), c, t, False).wait_send()


def body(x, gs, gt, gm, wqkv, logit, wps, wqv, codes, quantum, steps, wpt, w1, w2):
    n_p = lax.axis_size("patch")
    n_f = lax.axis_size("frame")
    _, rows, width = x.shape
    chunks = 4
    cs = wqkv.shape[2]
    ct = wqv.shape[2]
    ff = w1.shape[1]
    lane = np.arange(ct) % HW
    half = HW // 2
    partner = np.arange(ct) + np.where(lane < half, half, -half)
    swap = np.zeros((ct, ct), np.float32)
    swap[partner, np.arange(ct)] = 1.0
    same_t = (np.arange(ct)[:, None] // HW == np.arange(ct)[None] // HW).astype(np.float32)
    same_s = (np.arange(cs)[:, None] // HW == np.arange(cs)[None] // HW).astype(np.float32)
    inv = np.exp((np.arange(ct) % half).astype(np.float32) * np.float32(-2.0 * math.log(10000.0) / HW))
    sign = np.where(lane < half, -1.0, 1.0)
    dma = pltpu.SemaphoreType.DMA
    smem = pl.BlockSpec(memory_space=pltpu.SMEM)
    vmem = pl.BlockSpec(memory_space=pltpu.VMEM)
    hbm = pl.BlockSpec(memory_space=pl.ANY)
    n_x = n_p // 2
    V = pltpu.VMEM
    out = pl.pallas_call(
        functools.partial(kernel, (n_p, n_f, rows, chunks, cs, ct)),
        out_shape=jax.ShapeDtypeStruct((rows, width), F32),
        in_specs=[smem] * 3 + [hbm] * 2 + [vmem] * 8 + [hbm] * 6,
        out_specs=vmem,
        scratch_shapes=[
            V((rows, width), F32), V((rows, width), jnp.int32),
            V((3, width, cs), BF), V((n_p, cs, width), BF), V((2, width, ct), BF),
            V((n_f, ct, width), BF), V((width, ff), BF), V((ff, width), BF), dma((8,)),
            V((n_p, rows, width), BF), V((n_p, rows, cs), BF), V((n_p, rows, cs), BF),
            V((n_p, rows, cs), BF), V((n_p, rows, cs), BF), V((n_p, rows, cs), BF),
            V((n_f, rows, ct), BF), V((n_f, rows, ct), BF), V((n_f, rows, width), BF),
            V((n_f, rows, ct), BF), V((n_f, rows, ct), BF), V((n_f, rows, ct), BF), V((n_f, rows, ct), BF),
            V((rows, width), F32), V((n_p, rows, width), BF),
            V((n_x, rows, width), BF), V((n_x, rows, width), BF),
            V((n_x, rows, width), BF), V((n_x, rows, width), BF),
            dma((n_x, chunks)), dma((n_p, chunks)), dma((n_x, chunks)),
            dma((n_p,)), dma((n_p,)), dma((n_f,)), dma((n_f,)),
            dma((n_f, chunks)), dma((n_f, chunks)), dma((n_f, chunks)), dma((n_f, chunks)),
            dma((n_f,)), dma((n_f,)),
            dma((n_x, chunks)), dma((n_p, chunks)), dma((n_x, chunks)),
            dma((n_x,)), dma((n_x,)), dma((n_x,)), dma((n_x,)),
        ],
        compiler_params=pltpu.CompilerParams(
            collective_id=0, has_side_effects=True, vmem_limit_bytes=60 * 1024 * 1024),
    )(
        logit, quantum, steps, x[0], codes[0], gs[None], gt[None], gm[None],
        jnp.asarray(same_s, BF), jnp.asarray(same_t, BF), jnp.asarray(swap, BF),
        jnp.asarray(inv[None], F32), jnp.asarray(sign[None], F32),
        wqkv, wps.reshape(n_p, cs, width), wqv, wpt.reshape(n_f, ct, width), w1, w2,
    )
    return out[None]


def solution(mesh):
    in_specs = (
        P(("groups", "frame"), "patch", None),
        P(),
        P(),
        P(),
        P(None, None, "patch"),
        P(),
        P(),
        P(None, None, "frame"),
        P(("groups", "frame"), "patch", None),
        P(),
        P("groups"),
        P(),
        P(None, "patch"),
        P("patch", None),
    )
    out_specs = P(("groups", "frame"), "patch", None)
    return jax.shard_map(body, mesh=mesh, in_specs=in_specs, out_specs=out_specs, check_vma=False)
```

```python
import functools
import math

import jax
import jax.numpy as jnp
import numpy as np
from jax import lax
from jax.experimental import pallas as pl
from jax.experimental.pallas import tpu as pltpu
from jax.sharding import PartitionSpec as P

HEADS = 16
HW = 72
EPS = 1e-6
BF = jnp.bfloat16
F32 = jnp.float32
MESH = pl.DeviceIdType.MESH


def dot(a, b):
    return jnp.dot(a, b, preferred_element_type=F32)


def dot_nt(a, b):
    return lax.dot_general(a, b, (((1,), (1,)), ((), ())), preferred_element_type=F32)


def split_dot(a, b):
    high = a.astype(BF)
    low = (a - high.astype(F32)).astype(BF)
    return dot(high, b) + dot(low, b)


def rms(v, g):
    return (v * lax.rsqrt(jnp.mean(v * v, axis=-1, keepdims=True) + EPS) * g).astype(BF)


def hnorm(u, same):
    return u * lax.rsqrt(split_dot(u * u, same) * (1.0 / HW) + EPS)


def kernel(
    dims,
    logit_ref, quantum_ref, step_ref,
    x_hbm, codes_hbm, gs_ref, gt_ref, gm_ref,
    same_s_ref, same_t_ref, swap_ref, inv_ref, sign_ref,
    wqkv_hbm, wps_hbm, wqv_hbm, wpt_hbm, w1_hbm, w2_hbm,
    out_ref,
    x, codes, wqkv, wps, wqv, wpt, w1, w2, load_sem,
    tok_a, qs, ks, vs, att, att_in,
    kt_out, kt, tok_t, qt, vt, att_t, att_t_in,
    after, tok_m, sib_out, sib_in, x_out, x_in,
    a_send, a_recv, af_send,
    s_send, s_recv, k_send, k_recv,
    tl_send, tl_recv, tr_send, tr_recv, t_send, t_recv,
    m_send, m_recv, mf_send, b_send, b_recv, c_send, c_recv,
):
    n_p, n_f, rows, chunks, cs, ct = dims
    n_x = n_p // 2
    blocks = x_in.shape[1]
    wide = x_in.shape[3]
    me_g = lax.axis_index("groups")
    me_p = lax.axis_index("patch")
    me_f = lax.axis_index("frame")
    chip = lax.div(me_p, 2)
    core = lax.rem(me_p, 2)
    sib = me_p + 1 - 2 * core
    step_rows = rows // chunks

    def patch_dev(j):
        return (me_g, j, me_f)

    def frame_dev(j):
        return (me_g, me_p, j)

    loads = []
    for n, (src, dst) in enumerate(
        [(x_hbm, x), (codes_hbm, codes), (wqkv_hbm, wqkv), (wps_hbm, wps),
         (wqv_hbm, wqv), (wpt_hbm, wpt), (w1_hbm, w1), (w2_hbm, w2)]
    ):
        copy = pltpu.make_async_copy(src, dst, load_sem.at[n])
        copy.start()
        loads.append(copy)

    barrier = pltpu.get_barrier_semaphore()
    for d in range(1, n_p):
        pl.semaphore_signal(barrier, 1, device_id=patch_dev(lax.rem(me_p + d, n_p)), device_id_type=MESH)
    for d in range(1, n_f):
        pl.semaphore_signal(barrier, 1, device_id=frame_dev(lax.rem(me_f + d, n_f)), device_id_type=MESH)

    pending = []

    def send(src, dst, ssem, rsem, dev):
        copy = pltpu.make_async_remote_copy(
            src_ref=src, dst_ref=dst, send_sem=ssem, recv_sem=rsem,
            device_id=dev, device_id_type=MESH)
        copy.start()
        return copy

    def arrived(ref, rsem, ssem):
        pltpu.make_async_remote_copy(
            src_ref=ref, dst_ref=ref, send_sem=ssem, recv_sem=rsem,
            device_id=patch_dev(sib), device_id_type=MESH).wait_recv()

    def cut(c):
        return pl.ds(c * step_rows, step_rows)

    def gather_own(tok, ssem, rsem):
        for d in range(1, n_x):
            there = lax.rem(chip + d, n_x) * 2 + core
            for c in range(chunks):
                ref = tok.at[me_p, cut(c)]
                pending.append(send(ref, ref, ssem.at[d, c], rsem.at[me_p, c], patch_dev(there)))
        for c in range(chunks):
            ref = tok.at[me_p, cut(c)]
            pending.append(send(ref, ref, ssem.at[0, c], rsem.at[me_p, c], patch_dev(sib)))

    def wait_shard(tok, j, rsem, ssem):
        for c in range(chunks):
            arrived(tok.at[j, cut(c)], rsem.at[j, c], ssem.at[0, c])

    def forward(tok, d, ssem, rsem, fsem, which):
        j = lax.rem(chip + d, n_x) * 2 + core
        for c in which:
            ref = tok.at[j, cut(c)]
            arrived(ref, rsem.at[j, c], ssem.at[0, c])
            pending.append(send(ref, ref, fsem.at[d, c], rsem.at[j, c], patch_dev(sib)))

    loads[0].wait()
    tok_a[pl.ds(me_p, 1)] = rms(x[...], gs_ref[...].reshape(1, -1))[None]
    pl.semaphore_wait(barrier, n_p - 1 + n_f - 1)
    gather_own(tok_a, a_send, a_recv)

    same_s = same_s_ref[...]
    loads[2].wait()

    def pair(ref, xc):
        return ref[pl.ds(xc * 2, 2)].reshape(2 * rows, ref.shape[-1])

    def project(xc):
        t = pair(tok_a, xc)
        qs[pl.ds(xc * 2, 2)] = hnorm(dot_nt(t, wqkv[0]), same_s).astype(BF).reshape(2, rows, cs)
        ks[pl.ds(xc * 2, 2)] = hnorm(dot_nt(t, wqkv[1]), same_s).astype(BF).reshape(2, rows, cs)
        vs[pl.ds(xc * 2, 2)] = dot_nt(t, wqkv[2]).astype(BF).reshape(2, rows, cs)

    loads[1].wait()
    same_t = same_t_ref[...]
    swap = swap_ref[...]
    head_t = lax.broadcasted_iota(jnp.int32, (1, ct), 1)

    def angles(j):
        a = step_ref[j].astype(F32) * inv_ref[...]
        return jnp.cos(a), jnp.sin(a) * sign_ref[...]

    cos_me, sin_me = angles(me_f)
    heads_t = ct // HW
    for j in range(n_f):
        if j == n_f // 2:
            wait_shard(tok_a, sib, a_recv, a_send)
            project(chip)
            forward(tok_a, 1, a_send, a_recv, af_send, range(chunks - 1))
        u = codes[:, j * ct:(j + 1) * ct].astype(F32).astype(BF)
        scale = jnp.zeros((1, ct), F32)
        for h in range(heads_t):
            scale = jnp.where((head_t >= h * HW) & (head_t < (h + 1) * HW), quantum_ref[j * heads_t + h], scale)
        turned = u.astype(F32) * scale * cos_me + dot(u, swap) * scale * sin_me
        kt_out[j] = turned.astype(BF)
    for d in range(1, n_f):
        j = lax.rem(me_f + d, n_f)
        pending.append(send(kt_out.at[j], kt.at[me_f], k_send.at[d], k_recv.at[me_f], frame_dev(j)))
    kt[pl.ds(me_f, 1)] = kt_out[pl.ds(me_f, 1)]

    forward(tok_a, 1, a_send, a_recv, af_send, range(chunks - 1, chunks))
    for d in range(2, n_x):
        forward(tok_a, d, a_send, a_recv, af_send, range(chunks))
    for d in range(1, n_x):
        xc = lax.rem(chip + d, n_x)
        wait_shard(tok_a, xc * 2 + 1 - core, a_recv, a_send)
        project(xc)

    head_s = lax.broadcasted_iota(jnp.int32, (1, cs), 1)
    heads_s = cs // HW
    k_all = ks[...].reshape(n_p * rows, cs)
    v_all = vs[...].reshape(n_p * rows, cs)

    def attend(xc):
        q = pair(qs, xc)
        mixed = jnp.zeros((2 * rows, cs), F32)
        for h in range(heads_s):
            mine = (head_s >= h * HW) & (head_s < (h + 1) * HW)
            qh = jnp.where(mine, q, jnp.zeros_like(q))
            s = lax.dot_general(qh, k_all, (((1,), (1,)), ((), ())), preferred_element_type=F32)
            e = jnp.exp(s * (logit_ref[me_p * heads_s + h] * (1.0 / math.sqrt(HW))))
            p = (e * (1.0 / jnp.sum(e, axis=-1, keepdims=True))).astype(BF)
            mixed = jnp.where(mine, dot(p, v_all), mixed)
        att[pl.ds(xc * 2, 2)] = mixed.astype(BF).reshape(2, rows, cs)

    for d in range(1, n_x):
        xc = lax.rem(chip + d, n_x)
        attend(xc)
        for b in range(2):
            j = xc * 2 + b
            pending.append(send(att.at[j], att_in.at[me_p], s_send.at[2 * d + b], s_recv.at[me_p], patch_dev(j)))
    attend(chip)
    pending.append(send(att.at[sib], att_in.at[me_p], s_send.at[0], s_recv.at[me_p], patch_dev(sib)))
    att_in[pl.ds(me_p, 1)] = att[pl.ds(me_p, 1)]
    loads[3].wait()
    for d in range(1, n_p):
        j = lax.rem(me_p + d, n_p)
        arrived(att_in.at[j], s_recv.at[j], s_send.at[0])
    total = x[...]
    for j in range(n_p):
        total = total + dot(att_in[j], wps[j])
    after[...] = total

    tok_t[pl.ds(me_f, 1)] = rms(total, gt_ref[...].reshape(1, -1))[None]
    has_right = me_f + 1 < n_f
    has_left = me_f > 0
    late = []

    def pass_on(j, c, t, right):
        ref = tok_t.at[j, cut(c)]
        if right:
            return pltpu.make_async_remote_copy(
                src_ref=ref, dst_ref=ref, send_sem=tr_send.at[t, c], recv_sem=tr_recv.at[t, c],
                device_id=frame_dev(jnp.minimum(me_f + 1, n_f - 1)), device_id_type=MESH)
        return pltpu.make_async_remote_copy(
            src_ref=ref, dst_ref=ref, send_sem=tl_send.at[t, c], recv_sem=tl_recv.at[t, c],
            device_id=frame_dev(jnp.maximum(me_f - 1, 0)), device_id_type=MESH)

    for c in range(chunks):
        @pl.when(has_right)
        def _():
            pass_on(me_f, c, 0, True).start()

        @pl.when(has_left)
        def _():
            pass_on(me_f, c, 0, False).start()

    loads[4].wait()

    def project_t(j):
        t = tok_t[pl.ds(j, 1)].reshape(rows, tok_t.shape[-1])
        u = hnorm(dot_nt(t, wqv[0]), same_t)
        cos_j, sin_j = angles(j)
        qt[pl.ds(j, 1)] = (u * cos_j + split_dot(u, swap) * sin_j).astype(BF)[None]
        vt[pl.ds(j, 1)] = dot_nt(t, wqv[1]).astype(BF)[None]

    project_t(me_f)
    for t in range(1, n_f):
        from_left = me_f >= t
        from_right = me_f + t < n_f
        for c in range(chunks):
            @pl.when(from_left)
            def _():
                pass_on(jnp.maximum(me_f - t, 0), c, t - 1, True).wait_recv()

            if t < n_f - 1:
                @pl.when(from_left & has_right)
                def _():
                    pass_on(jnp.maximum(me_f - t, 0), c, t, True).start()

            @pl.when(from_right)
            def _():
                pass_on(jnp.minimum(me_f + t, n_f - 1), c, t - 1, False).wait_recv()

            if t < n_f - 1:
                @pl.when(from_right & has_left)
                def _():
                    pass_on(jnp.minimum(me_f + t, n_f - 1), c, t, False).start()

        @pl.when(from_left)
        def _():
            project_t(jnp.maximum(me_f - t, 0))

        @pl.when(from_right)
        def _():
            project_t(jnp.minimum(me_f + t, n_f - 1))

    for d in range(1, n_f):
        j = lax.rem(me_f + d, n_f)
        arrived(kt.at[j], k_recv.at[j], k_send.at[d])

    for d in sorted(range(n_f), key=lambda d: -min(d, n_f - d)):
        j = lax.rem(me_f + d, n_f)
        q = qt[pl.ds(j, 1)].reshape(rows, ct).astype(F32)
        prods = jnp.concatenate([q * kt[g].astype(F32) for g in range(n_f)], axis=0)
        e = jnp.exp(split_dot(prods, same_t) * (1.0 / math.sqrt(HW))).reshape(n_f, rows, ct)
        bottom = e[0]
        for g in range(1, n_f):
            bottom = bottom + e[g]
        inverse = 1.0 / bottom
        mixed = jnp.zeros((rows, ct), F32)
        for g in range(n_f):
            mixed = mixed + (e[g] * inverse).astype(BF).astype(F32) * vt[g].astype(F32)
        if d == 0:
            att_t_in[pl.ds(me_f, 1)] = mixed.astype(BF)[None]
        else:
            att_t[d] = mixed.astype(BF)
            pending.append(send(att_t.at[d], att_t_in.at[me_f], t_send.at[d], t_recv.at[me_f], frame_dev(j)))

    loads[5].wait()
    for d in range(1, n_f):
        j = lax.rem(me_f + d, n_f)
        arrived(att_t_in.at[j], t_recv.at[j], t_send.at[d])
    total = after[...]
    for j in range(n_f):
        total = total + dot(att_t_in[j], wpt[j])
    after[...] = total

    tok_m[pl.ds(me_p, 1)] = rms(total, gm_ref[...].reshape(1, -1))[None]
    gather_own(tok_m, m_send, m_recv)
    loads[6].wait()
    loads[7].wait()

    def widen(xc):
        u = dot(pair(tok_m, xc), w1[...])
        return (0.5 * u * (1.0 + lax.erf(u * (1.0 / math.sqrt(2.0))))).astype(BF)

    def part(both, which):
        return jnp.where(which == 0, both[:rows], both[rows:])

    def block(n):
        return pl.ds(n * wide, wide)

    wait_shard(tok_m, sib, m_recv, m_send)
    hidden = widen(chip)
    for d in range(1, n_x):
        forward(tok_m, d, m_send, m_recv, mf_send, range(chunks // 2))
    for n in range(blocks):
        both = dot(hidden, w2[:, block(n)])
        sib_out[0, n] = part(both, 1 - core).astype(BF)
        pending.append(send(sib_out.at[0, n], sib_in.at[0, n], b_send.at[0, n], b_recv.at[0, n], patch_dev(sib)))
        after[:, block(n)] = after[:, block(n)] + part(both, core)
    for d in range(1, n_x):
        forward(tok_m, d, m_send, m_recv, mf_send, range(chunks // 2, chunks))

    for d in range(1, n_x):
        xc = lax.rem(chip + d, n_x)
        wait_shard(tok_m, xc * 2 + 1 - core, m_recv, m_send)
        hidden = widen(xc)
        own = []

        def across(n):
            arrived(sib_in.at[d, n], b_recv.at[d, n], b_send.at[d, n])
            x_out[d, n] = (own[n] + sib_in[d, n].astype(F32)).astype(BF)
            pending.append(send(x_out.at[d, n], x_in.at[d, n], c_send.at[d, n], c_recv.at[d, n], patch_dev(xc * 2 + core)))

        for n in range(blocks):
            both = dot(hidden, w2[:, block(n)])
            sib_out[d, n] = part(both, 1 - core).astype(BF)
            pending.append(send(sib_out.at[d, n], sib_in.at[d, n], b_send.at[d, n], b_recv.at[d, n], patch_dev(sib)))
            own.append(part(both, core))
            if n > 0:
                across(n - 1)
        across(blocks - 1)
    for n in range(blocks):
        arrived(sib_in.at[0, n], b_recv.at[0, n], b_send.at[0, n])
        total = after[:, block(n)] + sib_in[0, n].astype(F32)
        for d in range(1, n_x):
            arrived(x_in.at[d, n], c_recv.at[d, n], c_send.at[d, n])
            total = total + x_in[d, n].astype(F32)
        out_ref[:, block(n)] = total

    for copy in pending:
        copy.wait_send()
    for t in range(n_f - 1):
        for c in range(chunks):
            @pl.when((me_f >= t) & has_right)
            def _():
                pass_on(jnp.maximum(me_f - t, 0), c, t, True).wait_send()

            @pl.when((me_f + t < n_f) & has_left)
            def _():
                pass_on(jnp.minimum(me_f + t, n_f - 1), c, t, False).wait_send()


def body(x, gs, gt, gm, wqkv, logit, wps, wqv, codes, quantum, steps, wpt, w1, w2):
    n_p = lax.axis_size("patch")
    n_f = lax.axis_size("frame")
    _, rows, width = x.shape
    chunks = 4
    blocks = 3
    cs = wqkv.shape[2]
    ct = wqv.shape[2]
    ff = w1.shape[1]
    lane = np.arange(ct) % HW
    half = HW // 2
    partner = np.arange(ct) + np.where(lane < half, half, -half)
    swap = np.zeros((ct, ct), np.float32)
    swap[partner, np.arange(ct)] = 1.0
    same_t = (np.arange(ct)[:, None] // HW == np.arange(ct)[None] // HW).astype(np.float32)
    same_s = (np.arange(cs)[:, None] // HW == np.arange(cs)[None] // HW).astype(np.float32)
    inv = np.exp((np.arange(ct) % half).astype(np.float32) * np.float32(-2.0 * math.log(10000.0) / HW))
    sign = np.where(lane < half, -1.0, 1.0)
    dma = pltpu.SemaphoreType.DMA
    smem = pl.BlockSpec(memory_space=pltpu.SMEM)
    vmem = pl.BlockSpec(memory_space=pltpu.VMEM)
    hbm = pl.BlockSpec(memory_space=pl.ANY)
    n_x = n_p // 2
    V = pltpu.VMEM
    out = pl.pallas_call(
        functools.partial(kernel, (n_p, n_f, rows, chunks, cs, ct)),
        out_shape=jax.ShapeDtypeStruct((rows, width), F32),
        in_specs=[smem] * 3 + [hbm] * 2 + [vmem] * 8 + [hbm] * 6,
        out_specs=vmem,
        scratch_shapes=[
            V((rows, width), F32), V((rows, width), jnp.int32),
            V((3, cs, width), BF), V((n_p, cs, width), BF), V((2, ct, width), BF),
            V((n_f, ct, width), BF), V((width, ff), BF), V((ff, width), BF), dma((8,)),
            V((n_p, rows, width), BF), V((n_p, rows, cs), BF), V((n_p, rows, cs), BF),
            V((n_p, rows, cs), BF), V((n_p, rows, cs), BF), V((n_p, rows, cs), BF),
            V((n_f, rows, ct), BF), V((n_f, rows, ct), BF), V((n_f, rows, width), BF),
            V((n_f, rows, ct), BF), V((n_f, rows, ct), BF), V((n_f, rows, ct), BF), V((n_f, rows, ct), BF),
            V((rows, width), F32), V((n_p, rows, width), BF),
            V((n_x, blocks, rows, width // blocks), BF), V((n_x, blocks, rows, width // blocks), BF),
            V((n_x, blocks, rows, width // blocks), BF), V((n_x, blocks, rows, width // blocks), BF),
            dma((n_x, chunks)), dma((n_p, chunks)), dma((n_x, chunks)),
            dma((n_p,)), dma((n_p,)), dma((n_f,)), dma((n_f,)),
            dma((n_f, chunks)), dma((n_f, chunks)), dma((n_f, chunks)), dma((n_f, chunks)),
            dma((n_f,)), dma((n_f,)),
            dma((n_x, chunks)), dma((n_p, chunks)), dma((n_x, chunks)),
            dma((n_x, blocks)), dma((n_x, blocks)), dma((n_x, blocks)), dma((n_x, blocks)),
        ],
        compiler_params=pltpu.CompilerParams(
            collective_id=0, has_side_effects=True, vmem_limit_bytes=60 * 1024 * 1024),
    )(
        logit, quantum, steps, x[0], codes[0], gs, gt, gm,
        jnp.asarray(same_s, BF), jnp.asarray(same_t, BF), jnp.asarray(swap, BF),
        jnp.asarray(inv[None], F32), jnp.asarray(sign[None], F32),
        jnp.swapaxes(wqkv, 1, 2), wps.reshape(n_p, cs, width), jnp.swapaxes(wqv, 1, 2), wpt.reshape(n_f, ct, width), w1, w2,
    )
    return out[None]


def solution(mesh):
    in_specs = (
        P(("groups", "frame"), "patch", None),
        P(),
        P(),
        P(),
        P(None, None, "patch"),
        P(),
        P(),
        P(None, None, "frame"),
        P(("groups", "frame"), "patch", None),
        P(),
        P("groups"),
        P(),
        P(None, "patch"),
        P("patch", None),
    )
    out_specs = P(("groups", "frame"), "patch", None)
    return jax.shard_map(body, mesh=mesh, in_specs=in_specs, out_specs=out_specs, check_vma=False)
```
